512 devices in a mesh: row: 32 (over y, x), col: 16 (over z, core).
Axes of the slice: x: 4, y: 8, z: 8, core: 2. Of those that a mesh axis runs over, the one named last changes fastest.
Arguments:
- tokens: int32 [256], replicated, may hold values from 0 to 8191
- emission_table: bfloat16 [8192, 32768], P('row', 'col'), may hold values from -3 to 0
- forward_rows: bfloat16 [256, 32768], P('col', 'row'), may hold values from 0.05 to 64
- backward_rows: bfloat16 [256, 32768], P('row', 'col'), may hold values from 0.05 to 64
- src_embed: bfloat16 [32768, 256], P(('row', 'col')), may hold values from -12 to 12
- tgt_embed: bfloat16 [32768, 256], P(('col', 'row')), may hold values from -12 to 12
Outputs:
- grad_src: float32 [32768, 256], P(('row', 'col'))
- grad_tgt: float32 [32768, 256], P(('col', 'row'))
The draws below stay inside these ranges and needn't reach their ends.
All inputs are finite; a program needn't handle non-finite values.
Results may differ from the reference program's by a relative error of at most 0.018.
Values may be sent and summed in bfloat16 or wider, within the bound.
No kernel may reach another device: no remote copies, remote signals or barrier semaphores. Data moves between devices by JAX's collectives and lax.ppermute only.
A program may use at most 64 MiB of HBM per device.

```python
import math
import jax
import jax.numpy as jnp
import numpy as np
from jax import lax

S = 32768
E = 256
VOCAB = 8192
SEQS = 256


def embed_pair(key):
    key_src, key_tgt, key_row, key_col = jax.random.split(key, 4)
    src = jnp.clip(0.35 * jax.random.normal(key_src, (S, E), jnp.float32), -2.1, 2.1)
    tgt = jnp.clip(0.35 * jax.random.normal(key_tgt, (S, E), jnp.float32), -2.1, 2.1)
    state_index = jnp.arange(S, dtype=jnp.float32)
    upper_part = (state_index >= float(S - S // 4)).astype(jnp.float32)
    lift_size = 2.0 / math.sqrt(E)
    tgt = tgt * (1.0 + 0.3 * upper_part)[:, None] + lift_size * upper_part[:, None]
    src_wave = 1.5 * jnp.cos(2.0 * math.pi * state_index / float(S // 8))
    src = src + lift_size * src_wave[:, None]
    stride = S // 8
    anchor_src = jnp.arange(8, dtype=jnp.int32) * stride + jax.random.randint(key_row, (8,), 0, stride)
    anchor_tgt = jnp.arange(8, dtype=jnp.int32) * stride + jax.random.randint(key_col, (8,), 0, stride - 1)
    tgt = tgt.at[anchor_tgt].set(tgt[anchor_tgt])
    src = src.at[anchor_src].set(src[anchor_src])
    tgt = tgt.at[anchor_tgt + 1].set(tgt[anchor_tgt + 1])
    return (src, tgt)


def rising_rows(key, row_low, row_high):
    key_base, key_row, key_state = jax.random.split(key, 3)
    base = jnp.exp(jax.random.uniform(key_base, (SEQS, S), jnp.float32, math.log(0.6), math.log(1.6)))
    rise = 1.0 + 2.0 * jnp.arange(S, dtype=jnp.float32) / S
    state_scale = jnp.exp(jax.random.uniform(key_state, (1, S), jnp.float32, math.log(0.2), math.log(5.0)))
    row_scale = jnp.exp(jax.random.uniform(key_row, (SEQS, 1), jnp.float32, math.log(row_low), math.log(row_high)))
    return base * rise[None, :] * state_scale * row_scale


def draw_forward_rows(key, part):
    key = jax.random.fold_in(key, 5)
    row_low, row_high = (1.0, 1.0)
    return rising_rows(key, row_low, row_high).astype(jnp.bfloat16)


def draw_backward_rows(key, part):
    key = jax.random.fold_in(key, 7)
    row_low, row_high = (1.0, 1.0)
    return rising_rows(key, row_low, row_high).astype(jnp.bfloat16)


def draw_src_embed(key, part):
    src, tgt = embed_pair(key)
    return src.astype(jnp.bfloat16)


def draw_tgt_embed(key, part):
    src, tgt = embed_pair(key)
    return tgt.astype(jnp.bfloat16)


def touch_ends(values, rng, low, largest):
    longest = values.shape.index(max(values.shape))
    spots = []
    for shift in (0, 1):
        where = [jax.random.randint(jax.random.fold_in(rng, axis), (), 0, length) for axis, length in enumerate(values.shape)]
        where[longest] = (where[longest] + shift) % values.shape[longest]
        spots.append(tuple(where))
    return values.at[spots[0]].set(low).at[spots[1]].set(largest)


def levels(stream_key, extent, shards, smallest, largest):
    level = 1.0
    for dim, parts in shards:
        heights = jax.random.uniform(jax.random.fold_in(jax.random.fold_in(stream_key, 6), dim), (parts,), jnp.float32, smallest / len(shards), largest / len(shards))
        level = level * jnp.repeat(jnp.exp(heights), extent[dim] // parts).reshape((-1,) + (1,) * (len(extent) - 1 - dim))
    return level


def cumulative_ranks(number_of, skew):
    loads = [(1 << 20) // math.isqrt(grade ** skew) + 1 for grade in range(1, number_of + 1)]
    scale = 1 + sum(loads) // (1 << 30)
    return np.cumsum(np.array([max(1, weight // scale) for weight in loads]))


def ranked_ids(key, dims, number_of, lean):
    grid = cumulative_ranks(number_of, lean)
    ticket = jax.random.randint(jax.random.fold_in(key, 1), dims, 0, int(grid[number_of - 1]))
    standing = jnp.searchsorted(jnp.asarray(grid, jnp.int32), ticket, side="right")
    return jax.random.permutation(jax.random.fold_in(key, 2), number_of)[standing].astype(jnp.int32)


def setup_inputs(seed: int = 0) -> dict:
    splits = jax.random.split(jax.random.key(seed), 7)
    tokens = touch_ends(ranked_ids(splits[0], (SEQS,), VOCAB, 2), jax.random.fold_in(splits[0], 3), 0, VOCAB - 1).astype(jnp.int32)
    emission_table = jnp.clip(-3.0 + 3.0 * jax.random.uniform(splits[1], (VOCAB, S), jnp.float32) ** levels(splits[1], (VOCAB, S), ((0, 32), (1, 16)), -0.2, 0.2), -3.0, 0.0).astype(jnp.bfloat16)
    forward_rows = draw_forward_rows(jax.random.fold_in(splits[6], 71), 0)
    backward_rows = draw_backward_rows(jax.random.fold_in(splits[6], 71), 0)
    src_embed = draw_src_embed(jax.random.fold_in(splits[6], 71), 0)
    tgt_embed = draw_tgt_embed(jax.random.fold_in(splits[6], 71), 0)
    return {"tokens": tokens, "emission_table": emission_table, "forward_rows": forward_rows, "backward_rows": backward_rows, "src_embed": src_embed, "tgt_embed": tgt_embed}


def exp_rows(src_rows, tgt_embed):
    logits = lax.dot_general(src_rows, tgt_embed, (((1,), (1,)), ((), ())), preferred_element_type=jnp.float32)
    row_peak = jnp.max(logits, axis=1)
    exp_full = jnp.exp(logits - row_peak[:, None])
    return jnp.sum(exp_full, axis=1), exp_full.astype(jnp.bfloat16)


def reference(tokens, emission_table, forward_rows, backward_rows, src_embed, tgt_embed):
    rows_size = min(512, S)
    num_blocks = S // rows_size
    looked = jnp.take(emission_table, tokens, axis=0).astype(jnp.float32)
    weighted = (jnp.exp(looked) * backward_rows.astype(jnp.float32)).astype(jnp.bfloat16)
    src_blocks = src_embed.reshape(num_blocks, rows_size, E)

    def first_pass(src_rows):
        row_sums, exp_block = exp_rows(src_rows, tgt_embed)
        reach = lax.dot_general(weighted, exp_block, (((1,), (1,)), ((), ())), preferred_element_type=jnp.float32)
        return row_sums, reach

    totals, reaches = lax.map(first_pass, src_blocks)
    forward_blocks = forward_rows.astype(jnp.float32).reshape(SEQS, num_blocks, rows_size).transpose(1, 0, 2)
    norm_terms = jnp.sum(forward_blocks * reaches / totals[:, None, :], axis=(0, 2))
    factor = jnp.float32(S) / jnp.float32(SEQS)

    def second_pass(acc_tgt, inputs):
        src_rows, forward_block, row_sums = inputs
        unused, exp_block = exp_rows(src_rows, tgt_embed)
        coeffs = (factor * forward_block / (norm_terms[:, None] * row_sums[None, :])).astype(jnp.bfloat16)
        summed = lax.dot_general(coeffs, weighted, (((0,), (0,)), ((), ())), preferred_element_type=jnp.float32)
        exp_wide = exp_block.astype(jnp.float32)
        counts = exp_wide * summed
        row_counts = jnp.sum(counts, axis=1)
        grad_logits = (counts - exp_wide * (row_counts / row_sums)[:, None]).astype(jnp.bfloat16)
        grad_rows = jnp.dot(grad_logits, tgt_embed, preferred_element_type=jnp.float32)
        acc_tgt = acc_tgt + lax.dot_general(grad_logits, src_rows, (((0,), (0,)), ((), ())), preferred_element_type=jnp.float32)
        return acc_tgt, grad_rows

    grad_tgt, grad_blocks = lax.scan(second_pass, jnp.zeros((S, E), jnp.float32), (src_blocks, forward_blocks, totals))
    return grad_blocks.reshape(S, E), grad_tgt
```

```python
import jax
import jax.numpy as jnp
from jax import lax
from jax.sharding import PartitionSpec as P

S = 32768
SEQS = 256
ROWS = 32
COLS = 16
BF = jnp.bfloat16
F32 = jnp.float32


def gather_by(x, axis, n):
    return lax.all_to_all(jnp.broadcast_to(x[None], (n,) + x.shape), axis, 0, 0)


def halving_sum(parts):
    me = lax.axis_index("col")
    held = parts
    for bit in range(4):
        pairs = held.reshape((held.shape[0] // 2, 2) + held.shape[1:])
        mine = (me >> bit) & 1
        kept = jnp.where(mine == 0, pairs[:, 0], pairs[:, 1])
        sent = jnp.where(mine == 0, pairs[:, 1], pairs[:, 0]).astype(BF)
        got = lax.ppermute(sent, "col", [(k, k ^ (1 << bit)) for k in range(COLS)])
        held = kept + got.astype(F32)
    return held[0]


def on_device(tokens, emission_table, forward_rows, backward_rows, src_embed, tgt_embed):
    vocab_local = emission_table.shape[0]
    offset = lax.axis_index("row") * vocab_local
    onehot = (tokens[:, None] == offset + jnp.arange(vocab_local, dtype=jnp.int32)[None, :]).astype(BF)
    looked = jnp.dot(onehot, emission_table, preferred_element_type=F32).astype(BF)
    width = tgt_embed.shape[1]
    own = SEQS // ROWS
    looked = looked.reshape(ROWS, own, -1, width).transpose(0, 2, 1, 3).reshape(ROWS, -1, width)
    depth = looked.shape[1]
    sent = jnp.concatenate([looked, jnp.broadcast_to(tgt_embed[None], (ROWS,) + tgt_embed.shape)], axis=1)
    both = lax.all_to_all(sent, "row", 0, 0)
    tgt_block = both[:, depth:].reshape(-1, width)
    own_look = jnp.sum(both[:, :depth].astype(F32), axis=0)
    own_look = own_look.reshape(-1, own, width).transpose(1, 0, 2).reshape(own, -1)
    own_weighted = (jnp.exp(own_look) * backward_rows.astype(F32)).astype(BF)

    src_block = lax.all_gather(src_embed, "col", axis=0, tiled=True)
    forward_all = lax.all_gather(forward_rows, "col", axis=0, tiled=True)
    own_weighted, src_block, forward_all = lax.optimization_barrier((own_weighted, src_block, forward_all))
    weighted = gather_by(own_weighted, "row", ROWS).reshape(SEQS, -1)

    logits = lax.dot_general(src_block, tgt_block, (((1,), (1,)), ((), ())), preferred_element_type=F32)
    local_peak = jnp.max(logits, axis=1)
    exp_full = jnp.exp(logits - local_peak[:, None])
    local_sums = jnp.sum(exp_full, axis=1)
    exp_block = exp_full.astype(BF)

    peaks_sums = lax.all_gather(jnp.stack([local_peak, local_sums]), "col")
    row_peak = jnp.max(peaks_sums[:, 0], axis=0)
    row_sums = jnp.sum(peaks_sums[:, 1] * jnp.exp(peaks_sums[:, 0] - row_peak[None]), axis=0)
    scale = jnp.exp(local_peak - row_peak)

    reach = lax.dot_general(weighted, exp_block, (((1,), (1,)), ((), ())), preferred_element_type=F32)
    share = reach * (scale / row_sums)[None, :]
    norm_terms = jnp.sum(forward_all.astype(F32) * share, axis=1)
    norm_terms = jnp.sum(gather_by(norm_terms, "col", COLS), axis=0)
    norm_terms = jnp.sum(gather_by(norm_terms, "row", ROWS), axis=0)
    forward_all = forward_all.astype(F32)
    factor = jnp.float32(S) / jnp.float32(SEQS)
    coeffs = (factor * forward_all / (norm_terms[:, None] * row_sums[None, :])).astype(BF)
    part = jnp.sum(coeffs.astype(F32) * share, axis=0)
    ratio = jnp.sum(gather_by(part, "col", COLS), axis=0)

    summed = lax.dot_general(coeffs, weighted, (((0,), (0,)), ((), ())), preferred_element_type=F32)
    grad_logits = (exp_block.astype(F32) * scale[:, None] * (summed - ratio[:, None])).astype(BF)
    tgt_part = lax.dot_general(grad_logits, src_block, (((0,), (0,)), ((), ())), preferred_element_type=F32)
    tgt_parts = lax.all_to_all(tgt_part.astype(BF).reshape((ROWS,) + tgt_embed.shape), "row", 0, 0)
    src_part = jnp.dot(grad_logits, tgt_block, preferred_element_type=F32)
    grad_src = halving_sum(src_part.reshape((COLS,) + src_embed.shape))
    grad_tgt = jnp.sum(tgt_parts.astype(F32), axis=0)
    return (grad_src, grad_tgt)


def solution(mesh):
    in_specs = (
        P(),
        P("row", "col"),
        P("col", "row"),
        P("row", "col"),
        P(("row", "col"), None),
        P(("col", "row"), None),
    )
    out_specs = (P(("row", "col"), None), P(("col", "row"), None))
    return jax.shard_map(
        on_device, mesh=mesh, in_specs=in_specs, out_specs=out_specs, check_vma=False
    )
```

```python
import jax
import jax.numpy as jnp
from jax import lax
from jax.sharding import PartitionSpec as P

S = 32768
SEQS = 256
ROWS = 32
COLS = 16
BF = jnp.bfloat16
F32 = jnp.float32


def gather_by(x, axis, n):
    return lax.all_to_all(jnp.broadcast_to(x[None], (n,) + x.shape), axis, 0, 0)


def halving_sum(parts):
    me = lax.axis_index("col")
    held = parts
    for bit in range(4):
        pairs = held.reshape((held.shape[0] // 2, 2) + held.shape[1:])
        mine = (me >> bit) & 1
        kept = jnp.where(mine == 0, pairs[:, 0], pairs[:, 1])
        sent = jnp.where(mine == 0, pairs[:, 1], pairs[:, 0]).astype(BF)
        got = lax.ppermute(sent, "col", [(k, k ^ (1 << bit)) for k in range(COLS)])
        held = kept + got.astype(F32)
    return held[0]


def on_device(tokens, emission_table, forward_rows, backward_rows, src_embed, tgt_embed):
    vocab_local = emission_table.shape[0]
    offset = lax.axis_index("row") * vocab_local
    onehot = (tokens[:, None] == offset + jnp.arange(vocab_local, dtype=jnp.int32)[None, :]).astype(BF)
    looked = jnp.dot(onehot, emission_table, preferred_element_type=F32).astype(BF)
    width = tgt_embed.shape[1]
    own = SEQS // ROWS
    looked = looked.reshape(ROWS, own, -1, width).transpose(0, 2, 1, 3).reshape(ROWS, -1, width)
    depth = looked.shape[1]
    sent = jnp.pad(looked, ((0, 0), (0, tgt_embed.shape[0]), (0, 0))) + jnp.pad(tgt_embed, ((depth, 0), (0, 0)))[None]
    both = lax.all_to_all(sent, "row", 0, 0)
    tgt_block = both[:, depth:].reshape(-1, width)
    own_look = jnp.sum(both[:, :depth].astype(F32), axis=0)
    own_look = own_look.reshape(-1, own, width).transpose(1, 0, 2).reshape(own, -1)
    own_weighted = (jnp.exp(own_look) * backward_rows.astype(F32)).astype(BF)

    src_block = lax.all_gather(src_embed, "col", axis=0, tiled=True)
    forward_all = lax.all_gather(forward_rows, "col", axis=0, tiled=True)
    own_weighted, src_block, forward_all = lax.optimization_barrier((own_weighted, src_block, forward_all))
    weighted = gather_by(own_weighted, "row", ROWS).reshape(SEQS, -1)

    logits = lax.dot_general(src_block, tgt_block, (((1,), (1,)), ((), ())), preferred_element_type=F32)
    local_peak = jnp.max(logits, axis=1)
    exp_full = jnp.exp(logits - local_peak[:, None])
    local_sums = jnp.sum(exp_full, axis=1)
    exp_block = exp_full.astype(BF)
    exp_block, local_sums = lax.optimization_barrier((exp_block, local_sums))

    peaks_sums = lax.all_gather(jnp.stack([local_peak, local_sums]), "col")
    row_peak = jnp.max(peaks_sums[:, 0], axis=0)
    row_sums = jnp.sum(peaks_sums[:, 1] * jnp.exp(peaks_sums[:, 0] - row_peak[None]), axis=0)
    scale = jnp.exp(local_peak - row_peak)

    reach = lax.dot_general(weighted, exp_block, (((1,), (1,)), ((), ())), preferred_element_type=F32)
    share = reach * (scale / row_sums)[None, :]
    norm_terms = jnp.sum(forward_all.astype(F32) * share, axis=1)
    norm_terms = jnp.sum(gather_by(norm_terms, "col", COLS), axis=0)
    norm_terms = jnp.sum(gather_by(norm_terms, "row", ROWS), axis=0)
    forward_all = forward_all.astype(F32)
    factor = jnp.float32(S) / jnp.float32(SEQS)
    coeffs = (factor * forward_all / (norm_terms[:, None] * row_sums[None, :])).astype(BF)
    part = jnp.sum(coeffs.astype(F32) * share, axis=0)
    ratio = jnp.sum(gather_by(part, "col", COLS), axis=0)

    summed = lax.dot_general(coeffs, weighted, (((0,), (0,)), ((), ())), preferred_element_type=F32)
    grad_logits = (exp_block.astype(F32) * scale[:, None] * (summed - ratio[:, None])).astype(BF)
    tgt_part = lax.dot_general(grad_logits, src_block, (((0,), (0,)), ((), ())), preferred_element_type=F32)
    tgt_parts = lax.all_to_all(tgt_part.astype(BF).reshape((ROWS,) + tgt_embed.shape), "row", 0, 0)
    src_part = jnp.dot(grad_logits, tgt_block, preferred_element_type=F32)
    grad_src = halving_sum(src_part.reshape((COLS,) + src_embed.shape))
    grad_tgt = jnp.sum(tgt_parts.astype(F32), axis=0)
    return (grad_src, grad_tgt)


def solution(mesh):
    in_specs = (
        P(),
        P("row", "col"),
        P("col", "row"),
        P("row", "col"),
        P(("row", "col"), None),
        P(("col", "row"), None),
    )
    out_specs = (P(("row", "col"), None), P(("col", "row"), None))
    return jax.shard_map(
        on_device, mesh=mesh, in_specs=in_specs, out_specs=out_specs, check_vma=False
    )
```

```python
import jax
import jax.numpy as jnp
from jax import lax
from jax.sharding import PartitionSpec as P

S = 32768
SEQS = 256
ROWS = 32
COLS = 16
BF = jnp.bfloat16
F32 = jnp.float32


def gather_by(x, axis, n):
    return lax.all_to_all(jnp.broadcast_to(x[None], (n,) + x.shape), axis, 0, 0)


def column_sum(kept, sent):
    me = lax.axis_index("col")
    held = kept + lax.ppermute(sent, "col", [(k, k ^ 1) for k in range(COLS)]).astype(F32)
    fours = held.reshape((4, -1) + held.shape[1:])
    mine = me >> 2
    total = lax.dynamic_index_in_dim(fours, mine, 0, keepdims=False)
    for d in (1, 2, 3):
        sent = lax.dynamic_index_in_dim(fours, mine ^ d, 0, keepdims=False).astype(BF)
        total = total + lax.ppermute(sent, "col", [(k, k ^ (4 * d)) for k in range(COLS)]).astype(F32)
    mine = (me >> 1) & 1
    last = 2
    kept = jnp.where(mine == 0, total[0], total[1])
    sent = jnp.where(mine == 0, total[1], total[0]).astype(BF)
    return kept + lax.ppermute(sent, "col", [(k, k ^ last) for k in range(COLS)]).astype(F32)


def on_device(tokens, emission_table, forward_rows, backward_rows, src_embed, tgt_embed):
    vocab_local = emission_table.shape[0]
    offset = lax.axis_index("row") * vocab_local
    onehot = (tokens[:, None] == offset + jnp.arange(vocab_local, dtype=jnp.int32)[None, :]).astype(BF)
    looked = jnp.dot(onehot, emission_table, preferred_element_type=F32).astype(BF)
    width = tgt_embed.shape[1]
    own = SEQS // ROWS
    looked = looked.reshape(ROWS, own, -1, width).transpose(0, 2, 1, 3).reshape(ROWS, -1, width)
    depth = looked.shape[1]
    sent = jnp.pad(looked, ((0, 0), (0, tgt_embed.shape[0]), (0, 0))) + jnp.pad(tgt_embed, ((depth, 0), (0, 0)))[None]
    both = lax.all_to_all(sent, "row", 0, 0)
    tgt_block = both[:, depth:].reshape(-1, width)
    own_look = jnp.sum(both[:, :depth].astype(F32), axis=0)
    own_look = own_look.reshape(-1, own, width).transpose(1, 0, 2).reshape(own, -1)
    own_weighted = (jnp.exp(own_look) * backward_rows.astype(F32)).astype(BF)

    src_block = lax.all_gather(src_embed, "col", axis=0, tiled=True)
    forward_all = lax.all_gather(forward_rows, "col", axis=0, tiled=True)
    own_weighted, src_block, forward_all = lax.optimization_barrier((own_weighted, src_block, forward_all))
    weighted = gather_by(own_weighted, "row", ROWS).reshape(SEQS, -1)

    logits = lax.dot_general(src_block, tgt_block, (((1,), (1,)), ((), ())), preferred_element_type=F32)
    local_peak = jnp.max(logits, axis=1)
    exp_full = jnp.exp(logits - local_peak[:, None])
    local_sums = jnp.sum(exp_full, axis=1)
    exp_block = exp_full.astype(BF)
    exp_block, local_sums = lax.optimization_barrier((exp_block, local_sums))

    peaks_sums = lax.all_gather(jnp.stack([local_peak, local_sums]), "col")
    row_peak = jnp.max(peaks_sums[:, 0], axis=0)
    row_sums = jnp.sum(peaks_sums[:, 1] * jnp.exp(peaks_sums[:, 0] - row_peak[None]), axis=0)
    scale = jnp.exp(local_peak - row_peak)

    reach = lax.dot_general(weighted, exp_block, (((1,), (1,)), ((), ())), preferred_element_type=F32)
    share = reach * (scale / row_sums)[None, :]
    norm_terms = jnp.sum(forward_all.astype(F32) * share, axis=1)
    norm_terms = jnp.sum(gather_by(norm_terms, "col", COLS), axis=0)
    norm_terms = jnp.sum(gather_by(norm_terms, "row", ROWS), axis=0)
    forward_all = forward_all.astype(F32)
    factor = jnp.float32(S) / jnp.float32(SEQS)
    coeffs = (factor * forward_all / (norm_terms[:, None] * row_sums[None, :])).astype(BF)
    part = jnp.sum(coeffs.astype(F32) * share, axis=0)
    ratio = jnp.sum(gather_by(part, "col", COLS), axis=0)

    summed = lax.dot_general(coeffs, weighted, (((0,), (0,)), ((), ())), preferred_element_type=F32)
    grad_logits = (exp_block.astype(F32) * scale[:, None] * (summed - ratio[:, None])).astype(BF)
    src_part = jnp.dot(grad_logits, tgt_block, preferred_element_type=F32)
    pairs = src_part.reshape((COLS // 2, 2) + src_embed.shape)
    mine = lax.axis_index("col") & 1
    kept = jnp.where(mine == 0, pairs[:, 0], pairs[:, 1])
    sent = jnp.where(mine == 0, pairs[:, 1], pairs[:, 0]).astype(BF)
    kept, sent, grad_logits = lax.optimization_barrier((kept, sent, grad_logits))
    grad_src = column_sum(kept, sent)
    tgt_part = lax.dot_general(grad_logits, src_block, (((0,), (0,)), ((), ())), preferred_element_type=F32)
    tgt_parts = lax.all_to_all(tgt_part.astype(BF).reshape((ROWS,) + tgt_embed.shape), "row", 0, 0)
    grad_tgt = jnp.sum(tgt_parts.astype(F32), axis=0)
    return (grad_src, grad_tgt)


def solution(mesh):
    in_specs = (
        P(),
        P("row", "col"),
        P("col", "row"),
        P("row", "col"),
        P(("row", "col"), None),
        P(("col", "row"), None),
    )
    out_specs = (P(("row", "col"), None), P(("col", "row"), None))
    return jax.shard_map(
        on_device, mesh=mesh, in_specs=in_specs, out_specs=out_specs, check_vma=False
    )
```

```python
import jax
import jax.numpy as jnp
from jax import lax
from jax.sharding import PartitionSpec as P

S = 32768
SEQS = 256
ROWS = 32
COLS = 16
XS = 4
YS = 8
ALONG_Y = [[y * XS + x for y in range(YS)] for x in range(XS)]
BF = jnp.bfloat16
F32 = jnp.float32


def gather_by(x, axis, n):
    return lax.all_to_all(jnp.broadcast_to(x[None], (n,) + x.shape), axis, 0, 0)


def column_sum(kept, sent):
    me = lax.axis_index("col")
    held = kept + lax.ppermute(sent, "col", [(k, k ^ 1) for k in range(COLS)]).astype(F32)
    fours = held.reshape((4, -1) + held.shape[1:])
    mine = me >> 2
    total = lax.dynamic_index_in_dim(fours, mine, 0, keepdims=False)
    for d in (1, 2, 3):
        sent = lax.dynamic_index_in_dim(fours, mine ^ d, 0, keepdims=False).astype(BF)
        total = total + lax.ppermute(sent, "col", [(k, k ^ (4 * d)) for k in range(COLS)]).astype(F32)
    mine = (me >> 1) & 1
    last = 2
    kept = jnp.where(mine == 0, total[0], total[1])
    sent = jnp.where(mine == 0, total[1], total[0]).astype(BF)
    return kept + lax.ppermute(sent, "col", [(k, k ^ last) for k in range(COLS)]).astype(F32)


def thirds(x):
    high = lax.reduce_precision(x, 8, 7)
    middle = lax.reduce_precision(x - high, 8, 7)
    return jnp.concatenate([high, middle, x - high - middle], axis=0).astype(BF)


def in_order(parts):
    x = lax.axis_index("row") % XS
    a, b, c, d = parts
    low = x & 1
    a, b, c, d = (jnp.where(low == 0, p, q) for p, q in ((a, b), (b, a), (c, d), (d, c)))
    high = x >> 1
    a, b, c, d = (jnp.where(high == 0, p, q) for p, q in ((a, c), (b, d), (c, a), (d, b)))
    return jnp.stack([a, b, c, d], axis=1)


def on_device(tokens, emission_table, forward_rows, backward_rows, src_embed, tgt_embed):
    vocab_local = emission_table.shape[0]
    offset = lax.axis_index("row") * vocab_local
    onehot = (tokens[:, None] == offset + jnp.arange(vocab_local, dtype=jnp.int32)[None, :]).astype(BF)
    looked = jnp.dot(onehot, emission_table, preferred_element_type=F32).astype(BF)
    width = tgt_embed.shape[1]
    own = SEQS // ROWS
    looks = lax.all_to_all(looked.reshape(ROWS, own, -1), "row", 0, 0)
    own_look = jnp.sum(looks.astype(F32), axis=0)
    own_weighted = (jnp.exp(own_look) * backward_rows.astype(F32)).astype(BF)

    held = lax.all_to_all(
        jnp.broadcast_to(tgt_embed[None], (YS,) + tgt_embed.shape), "row", 0, 0, axis_index_groups=ALONG_Y
    )
    others = [lax.ppermute(held, "row", [(k, k ^ d) for k in range(ROWS)]) for d in (1, 2, 3)]
    src_block = lax.all_gather(src_embed, "col", axis=0, tiled=True)
    *others, src_block = lax.optimization_barrier((*others, src_block))
    tgt_block = in_order([held] + others).reshape(-1, width)
    tgt_block, own_weighted = lax.optimization_barrier((tgt_block, own_weighted))
    weighted = gather_by(own_weighted, "row", ROWS).reshape(SEQS, -1)

    logits = lax.dot_general(src_block, tgt_block, (((1,), (1,)), ((), ())), preferred_element_type=F32)
    local_peak = jnp.max(logits, axis=1)
    exp_full = jnp.exp(logits - local_peak[:, None])
    local_sums = jnp.sum(exp_full, axis=1)
    exp_block = exp_full.astype(BF)
    exp_block, local_sums = lax.optimization_barrier((exp_block, local_sums))

    local = thirds(jnp.stack([local_peak, local_sums]))
    got = lax.all_gather(jnp.concatenate([forward_rows, local], axis=0), "col")
    forward_all = lax.optimization_barrier(got[:, : forward_rows.shape[0]].reshape(SEQS, -1))
    peaks_sums = got[:, forward_rows.shape[0] :].astype(F32)
    peaks_sums = (peaks_sums[:, :2] + peaks_sums[:, 2:4]) + peaks_sums[:, 4:]
    row_peak = jnp.max(peaks_sums[:, 0], axis=0)
    row_sums = jnp.sum(peaks_sums[:, 1] * jnp.exp(peaks_sums[:, 0] - row_peak[None]), axis=0)
    scale = jnp.exp(local_peak - row_peak)

    reach = lax.dot_general(weighted, exp_block, (((1,), (1,)), ((), ())), preferred_element_type=F32)
    share = reach * (scale / row_sums)[None, :]
    norm_terms = jnp.sum(forward_all.astype(F32) * share, axis=1)
    norm_terms = jnp.sum(gather_by(norm_terms, "col", COLS), axis=0)
    norm_terms = jnp.sum(gather_by(norm_terms, "row", ROWS), axis=0)
    forward_all = forward_all.astype(F32)
    factor = jnp.float32(S) / jnp.float32(SEQS)
    coeffs = (factor * forward_all / (norm_terms[:, None] * row_sums[None, :])).astype(BF)
    part = jnp.sum(coeffs.astype(F32) * share, axis=0)
    ratio = jnp.sum(gather_by(part, "col", COLS), axis=0)

    summed = lax.dot_general(coeffs, weighted, (((0,), (0,)), ((), ())), preferred_element_type=F32)
    grad_logits = (exp_block.astype(F32) * scale[:, None] * (summed - ratio[:, None])).astype(BF)
    src_part = jnp.dot(grad_logits, tgt_block, preferred_element_type=F32)
    pairs = src_part.reshape((COLS // 2, 2) + src_embed.shape)
    mine = lax.axis_index("col") & 1
    kept = jnp.where(mine == 0, pairs[:, 0], pairs[:, 1])
    sent = jnp.where(mine == 0, pairs[:, 1], pairs[:, 0]).astype(BF)
    kept, sent, grad_logits = lax.optimization_barrier((kept, sent, grad_logits))
    grad_src = column_sum(kept, sent)
    tgt_part = lax.dot_general(grad_logits, src_block, (((0,), (0,)), ((), ())), preferred_element_type=F32)
    tgt_parts = lax.all_to_all(tgt_part.astype(BF).reshape((ROWS,) + tgt_embed.shape), "row", 0, 0)
    grad_tgt = jnp.sum(tgt_parts.astype(F32), axis=0)
    return (grad_src, grad_tgt)


def solution(mesh):
    in_specs = (
        P(),
        P("row", "col"),
        P("col", "row"),
        P("row", "col"),
        P(("row", "col"), None),
        P(("col", "row"), None),
    )
    out_specs = (P(("row", "col"), None), P(("col", "row"), None))
    return jax.shard_map(
        on_device, mesh=mesh, in_specs=in_specs, out_specs=out_specs, check_vma=False
    )
```

```python
import jax
import jax.numpy as jnp
from jax import lax
from jax.sharding import PartitionSpec as P

S = 32768
SEQS = 256
ROWS = 32
COLS = 16
XS = 4
YS = 8
ALONG_Y = [[y * XS + x for y in range(YS)] for x in range(XS)]
BF = jnp.bfloat16
F32 = jnp.float32


def gather_by(x, axis, n):
    return lax.all_to_all(jnp.broadcast_to(x[None], (n,) + x.shape), axis, 0, 0)


def column_sum(kept, sent):
    me = lax.axis_index("col")
    held = kept + lax.ppermute(sent, "col", [(k, k ^ 1) for k in range(COLS)]).astype(F32)
    fours = held.reshape((4, -1) + held.shape[1:])
    mine = me >> 2
    total = lax.dynamic_index_in_dim(fours, mine, 0, keepdims=False)
    for d in (1, 2, 3):
        sent = lax.dynamic_index_in_dim(fours, mine ^ d, 0, keepdims=False).astype(BF)
        total = total + lax.ppermute(sent, "col", [(k, k ^ (4 * d)) for k in range(COLS)]).astype(F32)
    mine = (me >> 1) & 1
    last = 2
    kept = jnp.where(mine == 0, total[0], total[1])
    sent = jnp.where(mine == 0, total[1], total[0]).astype(BF)
    return kept + lax.ppermute(sent, "col", [(k, k ^ last) for k in range(COLS)]).astype(F32)


def thirds(x):
    high = lax.reduce_precision(x, 8, 7)
    middle = lax.reduce_precision(x - high, 8, 7)
    return jnp.concatenate([high, middle, x - high - middle], axis=0).astype(BF)


def in_order(parts):
    x = lax.axis_index("row") % XS
    a, b, c, d = parts
    low = x & 1
    a, b, c, d = (jnp.where(low == 0, p, q) for p, q in ((a, b), (b, a), (c, d), (d, c)))
    high = x >> 1
    a, b, c, d = (jnp.where(high == 0, p, q) for p, q in ((a, c), (b, d), (c, a), (d, b)))
    return jnp.stack([a, b, c, d], axis=1)


def on_device(tokens, emission_table, forward_rows, backward_rows, src_embed, tgt_embed):
    vocab_local = emission_table.shape[0]
    offset = lax.axis_index("row") * vocab_local
    onehot = (tokens[:, None] == offset + jnp.arange(vocab_local, dtype=jnp.int32)[None, :]).astype(BF)
    looked = jnp.dot(onehot, emission_table, preferred_element_type=F32).astype(BF)
    width = tgt_embed.shape[1]
    own = SEQS // ROWS
    looks = lax.all_to_all(looked.reshape(ROWS, own, -1), "row", 0, 0)
    own_look = jnp.sum(looks.astype(F32), axis=0)
    own_weighted = (jnp.exp(own_look) * backward_rows.astype(F32)).astype(BF)

    held = lax.all_to_all(
        jnp.broadcast_to(tgt_embed[None], (YS,) + tgt_embed.shape), "row", 0, 0, axis_index_groups=ALONG_Y
    )
    others = [lax.ppermute(held, "row", [(k, k ^ d) for k in range(ROWS)]) for d in (1, 2, 3)]
    src_block = lax.all_gather(src_embed, "col", axis=0, tiled=True)
    *others, src_block = lax.optimization_barrier((*others, src_block))
    tgt_block = in_order([held] + others).reshape(-1, width)
    tgt_block, own_weighted = lax.optimization_barrier((tgt_block, own_weighted))
    weighted = gather_by(own_weighted, "row", ROWS).reshape(SEQS, -1)

    logits = lax.dot_general(src_block, tgt_block, (((1,), (1,)), ((), ())), preferred_element_type=F32)
    local_peak = jnp.max(logits, axis=1)
    exp_full = jnp.exp(logits - local_peak[:, None])
    local_sums = jnp.sum(exp_full, axis=1)
    exp_block = exp_full.astype(BF)
    exp_block, local_sums = lax.optimization_barrier((exp_block, local_sums))

    local = thirds(jnp.stack([local_peak, local_sums]))
    got = lax.all_gather(jnp.concatenate([forward_rows, local], axis=0), "col")
    forward_all = lax.optimization_barrier(got[:, : forward_rows.shape[0]].reshape(SEQS, -1))
    peaks_sums = got[:, forward_rows.shape[0] :].astype(F32)
    peaks_sums = (peaks_sums[:, :2] + peaks_sums[:, 2:4]) + peaks_sums[:, 4:]
    row_peak = jnp.max(peaks_sums[:, 0], axis=0)
    row_sums = jnp.sum(peaks_sums[:, 1] * jnp.exp(peaks_sums[:, 0] - row_peak[None]), axis=0)
    scale = jnp.exp(local_peak - row_peak)

    reach = lax.dot_general(weighted, exp_block, (((1,), (1,)), ((), ())), preferred_element_type=F32)
    share = reach * (scale / row_sums)[None, :]
    kept_share = share.astype(BF)
    norm_terms = jnp.sum(forward_all.astype(F32) * share, axis=1)
    norm_terms = jnp.sum(gather_by(norm_terms, "col", COLS), axis=0)
    norm_terms = jnp.sum(gather_by(norm_terms, "row", ROWS), axis=0)
    forward_all = forward_all.astype(F32)
    factor = jnp.float32(S) / jnp.float32(SEQS)
    coeffs = (factor * forward_all / (norm_terms[:, None] * row_sums[None, :])).astype(BF)
    part = jnp.sum(coeffs.astype(F32) * kept_share.astype(F32), axis=0)
    ratio = jnp.sum(gather_by(part, "col", COLS), axis=0)

    summed = lax.dot_general(coeffs, weighted, (((0,), (0,)), ((), ())), preferred_element_type=F32)
    grad_logits = (exp_block.astype(F32) * scale[:, None] * (summed - ratio[:, None])).astype(BF)
    src_part = jnp.dot(grad_logits, tgt_block, preferred_element_type=F32)
    pairs = src_part.reshape((COLS // 2, 2) + src_embed.shape)
    mine = lax.axis_index("col") & 1
    kept = jnp.where(mine == 0, pairs[:, 0], pairs[:, 1])
    sent = jnp.where(mine == 0, pairs[:, 1], pairs[:, 0]).astype(BF)
    kept, sent, grad_logits = lax.optimization_barrier((kept, sent, grad_logits))
    grad_src = column_sum(kept, sent)
    tgt_part = lax.dot_general(grad_logits, src_block, (((0,), (0,)), ((), ())), preferred_element_type=F32)
    tgt_parts = lax.all_to_all(tgt_part.astype(BF).reshape((ROWS,) + tgt_embed.shape), "row", 0, 0)
    grad_tgt = jnp.sum(tgt_parts.astype(F32), axis=0)
    return (grad_src, grad_tgt)


def solution(mesh):
    in_specs = (
        P(),
        P("row", "col"),
        P("col", "row"),
        P("row", "col"),
        P(("row", "col"), None),
        P(("col", "row"), None),
    )
    out_specs = (P(("row", "col"), None), P(("col", "row"), None))
    return jax.shard_map(
        on_device, mesh=mesh, in_specs=in_specs, out_specs=out_specs, check_vma=False
    )
```

```python
import jax
import jax.numpy as jnp
from jax import lax
from jax.sharding import PartitionSpec as P

S = 32768
SEQS = 256
ROWS = 32
COLS = 16
XS = 4
YS = 8
ALONG_Y = [[y * XS + x for y in range(YS)] for x in range(XS)]
BF = jnp.bfloat16
F32 = jnp.float32


def gather_by(x, axis, n):
    return lax.all_to_all(jnp.broadcast_to(x[None], (n,) + x.shape), axis, 0, 0)


def column_sum(kept, sent):
    me = lax.axis_index("col")
    held = kept + lax.ppermute(sent, "col", [(k, k ^ 1) for k in range(COLS)]).astype(F32)
    fours = held.reshape((4, -1) + held.shape[1:])
    mine = me >> 2
    total = lax.dynamic_index_in_dim(fours, mine, 0, keepdims=False)
    for d in (1, 2, 3):
        sent = lax.dynamic_index_in_dim(fours, mine ^ d, 0, keepdims=False).astype(BF)
        total = total + lax.ppermute(sent, "col", [(k, k ^ (4 * d)) for k in range(COLS)]).astype(F32)
    mine = (me >> 1) & 1
    last = 2
    kept = jnp.where(mine == 0, total[0], total[1])
    sent = jnp.where(mine == 0, total[1], total[0]).astype(BF)
    return kept + lax.ppermute(sent, "col", [(k, k ^ last) for k in range(COLS)]).astype(F32)


def thirds(x):
    high = lax.reduce_precision(x, 8, 7)
    middle = lax.reduce_precision(x - high, 8, 7)
    return jnp.concatenate([high, middle, x - high - middle], axis=0).astype(BF)


def in_order(parts):
    x = lax.axis_index("row") % XS
    a, b, c, d = parts
    low = x & 1
    a, b, c, d = (jnp.where(low == 0, p, q) for p, q in ((a, b), (b, a), (c, d), (d, c)))
    high = x >> 1
    a, b, c, d = (jnp.where(high == 0, p, q) for p, q in ((a, c), (b, d), (c, a), (d, b)))
    return jnp.stack([a, b, c, d], axis=1)


def on_device(tokens, emission_table, forward_rows, backward_rows, src_embed, tgt_embed):
    vocab_local = emission_table.shape[0]
    offset = lax.axis_index("row") * vocab_local
    onehot = (tokens[:, None] == offset + jnp.arange(vocab_local, dtype=jnp.int32)[None, :]).astype(BF)
    looked = jnp.dot(onehot, emission_table, preferred_element_type=F32).astype(BF)
    width = tgt_embed.shape[1]
    own = SEQS // ROWS
    looks = lax.all_to_all(looked.reshape(ROWS, own, -1), "row", 0, 0)
    own_look = jnp.sum(looks.astype(F32), axis=0)
    own_weighted = (jnp.exp(own_look) * backward_rows.astype(F32)).astype(BF)

    held = lax.all_to_all(
        jnp.broadcast_to(tgt_embed[None], (YS,) + tgt_embed.shape), "row", 0, 0, axis_index_groups=ALONG_Y
    )
    others = [lax.ppermute(held, "row", [(k, k ^ d) for k in range(ROWS)]) for d in (1, 2, 3)]
    src_block = lax.all_gather(src_embed, "col", axis=0, tiled=True)
    *others, src_block = lax.optimization_barrier((*others, src_block))
    tgt_block = in_order([held] + others).reshape(-1, width)
    tgt_block, own_weighted = lax.optimization_barrier((tgt_block, own_weighted))
    weighted = gather_by(own_weighted, "row", ROWS).reshape(SEQS, -1)

    logits = lax.dot_general(src_block, tgt_block, (((1,), (1,)), ((), ())), preferred_element_type=F32)
    local_peak = jnp.max(logits, axis=1)
    exp_full = jnp.exp(logits - local_peak[:, None])
    local_sums = jnp.sum(exp_full, axis=1)
    exp_block = exp_full.astype(BF)
    exp_block, local_sums = lax.optimization_barrier((exp_block, local_sums))

    local = thirds(jnp.stack([local_peak, local_sums]))
    got = lax.all_gather(jnp.concatenate([forward_rows, local], axis=0), "col")
    forward_all = lax.optimization_barrier(got[:, : forward_rows.shape[0]].reshape(SEQS, -1))
    peaks_sums = got[:, forward_rows.shape[0] :].astype(F32)
    peaks_sums = (peaks_sums[:, :2] + peaks_sums[:, 2:4]) + peaks_sums[:, 4:]
    row_peak = jnp.max(peaks_sums[:, 0], axis=0)
    row_sums = jnp.sum(peaks_sums[:, 1] * jnp.exp(peaks_sums[:, 0] - row_peak[None]), axis=0)
    scale = jnp.exp(local_peak - row_peak)

    reach = lax.dot_general(weighted, exp_block, (((1,), (1,)), ((), ())), preferred_element_type=F32)
    share = reach * (scale / row_sums)[None, :]
    kept_share = share.astype(BF)
    norm_terms = jnp.sum(forward_all.astype(F32) * share, axis=1)
    norm_terms = jnp.sum(gather_by(norm_terms, "col", COLS), axis=0)
    norm_terms = jnp.sum(gather_by(norm_terms, "row", ROWS), axis=0)
    forward_all = forward_all.astype(F32)
    factor = jnp.float32(S) / jnp.float32(SEQS)
    coeffs = (factor * forward_all / (norm_terms[:, None] * row_sums[None, :])).astype(BF)
    part = jnp.sum(coeffs.astype(F32) * kept_share.astype(F32), axis=0)
    coeffs, part = lax.optimization_barrier((coeffs, part))
    ratio = jnp.sum(gather_by(part, "col", COLS), axis=0)

    summed = lax.dot_general(coeffs, weighted, (((0,), (0,)), ((), ())), preferred_element_type=F32)
    grad_logits = (exp_block.astype(F32) * scale[:, None] * (summed - ratio[:, None])).astype(BF)
    src_part = jnp.dot(grad_logits, tgt_block, preferred_element_type=F32)
    pairs = src_part.reshape((COLS // 2, 2) + src_embed.shape)
    mine = lax.axis_index("col") & 1
    kept = jnp.where(mine == 0, pairs[:, 0], pairs[:, 1])
    sent = jnp.where(mine == 0, pairs[:, 1], pairs[:, 0]).astype(BF)
    kept, sent, grad_logits = lax.optimization_barrier((kept, sent, grad_logits))
    grad_src = column_sum(kept, sent)
    tgt_part = lax.dot_general(grad_logits, src_block, (((0,), (0,)), ((), ())), preferred_element_type=F32)
    tgt_parts = lax.all_to_all(tgt_part.astype(BF).reshape((ROWS,) + tgt_embed.shape), "row", 0, 0)
    grad_tgt = jnp.sum(tgt_parts.astype(F32), axis=0)
    return (grad_src, grad_tgt)


def solution(mesh):
    in_specs = (
        P(),
        P("row", "col"),
        P("col", "row"),
        P("row", "col"),
        P(("row", "col"), None),
        P(("col", "row"), None),
    )
    out_specs = (P(("row", "col"), None), P(("col", "row"), None))
    return jax.shard_map(
        on_device, mesh=mesh, in_specs=in_specs, out_specs=out_specs, check_vma=False
    )
```
